32 devices in a mesh: rep: 2 (over core), fsdp: 16 (over z, y, x).
Axes of the slice: x: 2, y: 2, z: 4, core: 2. Of those that a mesh axis runs over, the one named last changes fastest.
Arguments:
- anchor: float32 [3584, 7168], P('fsdp'), may hold values from -6 to 6
- momentum: float32 [3584, 7168], P('fsdp', 'rep'), may hold values from -3 to 3
- inner_weight: float32 [2, 3584, 7168], P('rep', 'fsdp'), may hold values from -6 to 6
- first_moment: float32 [2, 3584, 7168], P('rep', 'fsdp'), may hold values from -2 to 2
- second_moment: float32 [2, 3584, 7168], P('rep', 'fsdp'), may hold values from 0.01 to 1
- grad_first: bfloat16 [2, 3584, 7168], P('rep', 'fsdp'), may hold values from -1100 to 1100
- grad_second: bfloat16 [2, 3584, 7168], P('rep', 'fsdp'), may hold values from -1100 to 1100
- outer_step: int32 [1], replicated, may hold values from 0 to 15
Outputs:
- next_anchor: float32 [3584, 7168], P('fsdp')
- next_momentum: float32 [3584, 7168], P('fsdp', 'rep')
- next_inner: float32 [2, 3584, 7168], P('rep', 'fsdp')
- next_first: float32 [2, 3584, 7168], P('rep', 'fsdp')
- next_second: float32 [2, 3584, 7168], P('rep', 'fsdp')
The draws below stay inside these ranges and needn't reach their ends.
All inputs are finite; a program needn't handle non-finite values.
Results may differ from the reference program's by a relative error of at most 0.0003.
Values sent between devices are 32-bit elements; how exact they have to be, the bound alone decides.
A program may use at most 128 MiB of HBM per device.

```python
import math
import jax
import jax.numpy as jnp

D = 3584
FF = 7168
REPS = 2
N_REP = 2


def grad_draw(key):
    subkeys = jax.random.split(key, 3)
    row_pos = jnp.arange(D, dtype=jnp.float32) / max(D - 1, 1)
    entries = jnp.clip(jax.random.normal(subkeys[0], (REPS, D, FF), jnp.float32), -4.0, 4.0)
    rising = 3.0
    row_scale = jnp.exp(jax.random.uniform(subkeys[1], (REPS, D, 1), jnp.float32) * math.log(10.0))
    row_scale = row_scale * jnp.power(rising, 0.5 * row_pos)[None, :, None]
    col_scale = jnp.exp(jax.random.uniform(subkeys[2], (REPS, 1, FF), jnp.float32) * math.log(10.0))
    return (entries * row_scale * col_scale).astype(jnp.bfloat16)


def draw_grad_first(key, part):
    return grad_draw(jax.random.fold_in(key, 11))


def draw_grad_second(key, part):
    return grad_draw(jax.random.fold_in(key, 12))


def levels(rng, extent, pieces, least, largest):
    def one(dim, blocks):
        heights = jax.random.uniform(jax.random.fold_in(jax.random.fold_in(rng, 6), dim), (blocks,), jnp.float32, least / len(pieces), largest / len(pieces))
        return jnp.repeat(jnp.exp(heights), extent[dim] // blocks).reshape((-1,) + (1,) * (len(extent) - dim - 1))

    level = one(*pieces[0])
    for cut in pieces[1:]:
        level = level * one(*cut)
    return level


def bell_draw(stream_key, shape, spread, reach, pieces=(), kind=jnp.bfloat16):
    gain = levels(stream_key, shape, pieces, -0.22, 0.18) if pieces else 1.0
    result = jax.random.normal(stream_key, shape, jnp.float32) * spread * gain
    return jnp.minimum(jnp.maximum(result, -reach), reach).astype(kind)


def setup_inputs(seed: int = 0) -> dict:
    seeds = jax.random.split(jax.random.key(seed), 9)
    return {
        "anchor": bell_draw(seeds[0], (D, FF), 1.0, 6.0, ((0, 16),), jnp.float32),
        "momentum": bell_draw(seeds[1], (D, FF), 0.5, 3.0, ((0, 16), (1, 2)), jnp.float32),
        "inner_weight": bell_draw(seeds[2], (REPS, D, FF), 1.0, 6.0, ((0, 2), (1, 16)), jnp.float32),
        "first_moment": bell_draw(seeds[3], (REPS, D, FF), 0.3, 2.0, ((0, 2), (1, 16)), jnp.float32),
        "second_moment": jnp.clip(jnp.exp(math.log(1.0) - 4.6051702 * jax.random.uniform(seeds[4], (REPS, D, FF), jnp.float32) ** levels(seeds[4], (REPS, D, FF), ((0, 2), (1, 16)), -0.2, 0.2)), 0.01, 1.0),
        "grad_first": draw_grad_first(jax.random.fold_in(seeds[8], 71), 0),
        "grad_second": draw_grad_second(jax.random.fold_in(seeds[8], 71), 0),
        "outer_step": jax.random.randint(seeds[7], (1,), 0, 16).astype(jnp.int32),
    }


def adam_step(weight, first_moment, second_moment, gradient, step_count):
    grad_full = gradient.astype(jnp.float32)
    square_sum = jnp.sum(grad_full * grad_full)
    factor = jnp.minimum(1.0, 0.5 * math.sqrt(D * FF) / (jnp.sqrt(square_sum) + 1e-06))
    scaled = factor * grad_full
    first_moment = 0.9 * first_moment + 0.1 * scaled
    second_moment = 0.95 * second_moment + 0.05 * scaled * scaled
    first_hat = first_moment / (1.0 - jnp.power(jnp.float32(0.9), step_count))
    second_hat = second_moment / (1.0 - jnp.power(jnp.float32(0.95), step_count))
    weight = weight - 0.1 * (first_hat / (jnp.sqrt(second_hat) + 1e-08) + 0.1 * weight)
    return (weight, first_moment, second_moment)

def reference(anchor, momentum, inner_weight, first_moment, second_moment, grad_first, grad_second, outer_step):
    pseudo_sum = jnp.zeros_like(anchor)
    for replica in range(N_REP):
        pseudo_sum = pseudo_sum + (anchor - inner_weight[replica])
    outer_grad = pseudo_sum / N_REP
    next_momentum = 0.9 * momentum + outer_grad
    next_anchor = anchor - 0.7 * (outer_grad + 0.9 * next_momentum)
    base_step = 2 * outer_step[0]
    inner_list, first_list, second_list = ([], [], [])
    for replica in range(N_REP):
        weight = inner_weight[replica]
        moment_one = first_moment[replica]
        moment_two = second_moment[replica]
        weight, moment_one, moment_two = adam_step(weight, moment_one, moment_two, grad_first[replica], (base_step + 1).astype(jnp.float32))
        weight, moment_one, moment_two = adam_step(weight, moment_one, moment_two, grad_second[replica], (base_step + 2).astype(jnp.float32))
        inner_list.append(next_anchor + (weight - inner_weight[replica]))
        first_list.append(moment_one)
        second_list.append(moment_two)
    return (next_anchor, next_momentum, jnp.stack(inner_list), jnp.stack(first_list), jnp.stack(second_list))
```

```python
import functools
import math

import jax
import jax.numpy as jnp
from jax import lax
from jax.experimental import pallas as pl
from jax.experimental.pallas import tpu as pltpu
from jax.sharding import PartitionSpec as P

D = 3584
FF = 7168
CHUNK = 32
ROWS = 16
COLS = 256
SLOTS = 4
MESH = pl.DeviceIdType.MESH


def adam_apply(weight, first_moment, second_moment, grad_full, square_sum, step_count):
    factor = jnp.minimum(1.0, 0.5 * math.sqrt(D * FF) / (jnp.sqrt(square_sum) + 1e-06))
    scaled = factor * grad_full
    first_moment = 0.9 * first_moment + 0.1 * scaled
    second_moment = 0.95 * second_moment + 0.05 * scaled * scaled
    first_hat = first_moment / (1.0 - jnp.power(jnp.float32(0.9), step_count))
    second_hat = second_moment / (1.0 - jnp.power(jnp.float32(0.95), step_count))
    weight = weight - 0.1 * (first_hat / (jnp.sqrt(second_hat) + 1e-08) + 0.1 * weight)
    return (weight, first_moment, second_moment)


def outer_update(anchor, momentum, inner_weight):
    replicas = lax.axis_size("rep")
    col_count = momentum.shape[1]
    col_start = lax.axis_index("rep") * col_count
    pseudo = anchor - inner_weight[0]
    pseudo_sum = lax.psum(pseudo, "rep")
    full_momentum = lax.all_gather(momentum, "rep", axis=1, tiled=True)
    outer_grad = pseudo_sum / replicas
    momentum_full = 0.9 * full_momentum + outer_grad
    next_anchor = anchor - 0.7 * (outer_grad + 0.9 * momentum_full)
    next_momentum = lax.dynamic_slice_in_dim(momentum_full, col_start, col_count, 1)
    return (next_anchor, next_momentum)


def inner_steps(inner_weight, first_moment, second_moment, grad_first, grad_second, outer_step):
    base_step = 2 * outer_step[0]
    grad_one = grad_first[0].astype(jnp.float32)
    grad_two = grad_second[0].astype(jnp.float32)
    weight, moment_one, moment_two = (inner_weight[0], first_moment[0], second_moment[0])
    for offset, grad_full in ((1, grad_one), (2, grad_two)):
        square_sum = lax.psum(jnp.sum(grad_full * grad_full), "fsdp")
        weight, moment_one, moment_two = adam_apply(
            weight,
            moment_one,
            moment_two,
            grad_full,
            square_sum,
            (base_step + offset).astype(jnp.float32),
        )
    return (weight, moment_one, moment_two)


def plain(
    anchor, momentum, inner_weight, first_moment, second_moment, grad_first, grad_second, outer_step
):
    weight, moment_one, moment_two = inner_steps(
        inner_weight, first_moment, second_moment, grad_first, grad_second, outer_step
    )
    next_anchor, next_momentum = outer_update(anchor, momentum, inner_weight)
    next_inner = (next_anchor + (weight - inner_weight[0]))[None]
    return (next_anchor, next_momentum, next_inner, moment_one[None], moment_two[None])


def exchange_kernel(
    peers,
    anchor, momentum, inner, first, second, grad_one, grad_two,
    na, nm, w, m, v, g1, g2, sums,
    other_w, gathered,
    g1_sem, g2_sem, a_sem, w_sem, mom_sem, bulk_sem,
    w_send, w_recv, na_send, na_recv, s_send, s_recv,
):
    rows, half = momentum.shape
    chunks = rows // CHUNK
    me = lax.axis_index("fsdp")
    rep = lax.axis_index("rep")
    partner = 1 - rep
    own = pl.ds(pl.multiple_of(rep * half, 128), half)
    far = pl.ds(pl.multiple_of(partner * half, 128), half)

    def cut(i):
        return pl.ds(i * CHUNK, CHUNK)

    barrier = pltpu.get_barrier_semaphore()
    pl.semaphore_signal(barrier, inc=1, device_id={"rep": partner}, device_id_type=MESH)
    for d in range(1, peers):
        pl.semaphore_signal(
            barrier, inc=1, device_id={"fsdp": lax.rem(me + d, peers)}, device_id_type=MESH
        )

    g1_in = [pltpu.make_async_copy(grad_one.at[0, cut(i)], g1.at[cut(i)], g1_sem.at[i]) for i in range(chunks)]
    g2_in = [pltpu.make_async_copy(grad_two.at[0, cut(i)], g2.at[cut(i)], g2_sem.at[i]) for i in range(chunks)]
    a_in = [pltpu.make_async_copy(anchor.at[cut(i), own], na.at[cut(i), own], a_sem.at[i]) for i in range(chunks)]
    w_in = [pltpu.make_async_copy(inner.at[0, cut(i), own], w.at[cut(i), own], w_sem.at[i]) for i in range(chunks)]
    mom_in = [pltpu.make_async_copy(momentum.at[cut(i)], nm.at[cut(i)], mom_sem.at[i]) for i in range(chunks)]
    bulk = [
        pltpu.make_async_copy(inner.at[0, :, far], w.at[:, far], bulk_sem.at[0]),
        pltpu.make_async_copy(first.at[0], m, bulk_sem.at[1]),
        pltpu.make_async_copy(second.at[0], v, bulk_sem.at[2]),
    ]
    for i in range(chunks):
        g1_in[i].start()
        g2_in[i].start()
    for i in range(chunks):
        a_in[i].start()
        w_in[i].start()
        mom_in[i].start()

    pl.semaphore_wait(barrier, peers)

    w_out = [
        pltpu.make_async_remote_copy(
            src_ref=inner.at[0, cut(i), far], dst_ref=other_w.at[cut(i)],
            send_sem=w_send.at[i], recv_sem=w_recv.at[i],
            device_id={"rep": partner}, device_id_type=MESH,
        )
        for i in range(chunks)
    ]
    for c in w_out:
        c.start()
    for c in bulk:
        c.start()

    lane = 128
    tiles = (2 * half) // lane
    total1 = total2 = jnp.zeros((8, lane), jnp.float32)
    for i in range(chunks):
        g1_in[i].wait()
        g2_in[i].wait()

        def square(j, carry):
            base = pl.multiple_of(i * CHUNK + j * ROWS, ROWS)
            accs = list(carry)
            for t in range(tiles):
                for k, ref in ((0, g1), (2, g2)):
                    x = ref[pl.ds(base, ROWS), t * lane:(t + 1) * lane].astype(jnp.float32)
                    x = x * x
                    accs[k] = accs[k] + x[:8]
                    accs[k + 1] = accs[k + 1] + x[8:]
            return tuple(accs)

        zero = jnp.zeros((8, lane), jnp.float32)
        accs = lax.fori_loop(0, CHUNK // ROWS, square, (zero,) * 4)
        total1 = total1 + (accs[0] + accs[1])
        total2 = total2 + (accs[2] + accs[3])

    gathered[me, 0] = total1
    gathered[me, 1] = total2
    s_out = []
    for d in range(1, peers):
        c = pltpu.make_async_remote_copy(
            src_ref=gathered.at[me], dst_ref=gathered.at[me],
            send_sem=s_send.at[d], recv_sem=s_recv.at[me],
            device_id={"fsdp": lax.rem(me + d, peers)}, device_id_type=MESH,
        )
        c.start()
        s_out.append(c)

    na_out = []
    for i in range(chunks):
        a_in[i].wait()
        w_in[i].wait()
        mom_in[i].wait()
        w_out[i].wait_recv()

        def outer(j, carry):
            base = pl.multiple_of(i * CHUNK + j * 8, 8)
            rs = pl.ds(base, 8)
            for t in range(0, half, COLS):
                cs = pl.ds(pl.multiple_of(rep * half + t, 128), COLS)
                a = na[rs, cs]
                grad = ((a - w[rs, cs]) + (a - other_w[rs, t:t + COLS])) * 0.5
                mom = 0.9 * nm[rs, t:t + COLS] + grad
                nm[rs, t:t + COLS] = mom
                na[rs, cs] = a - 0.7 * (grad + 0.9 * mom)
            return carry

        lax.fori_loop(0, CHUNK // 8, outer, 0)
        c = pltpu.make_async_remote_copy(
            src_ref=na.at[cut(i), own], dst_ref=na.at[cut(i), own],
            send_sem=na_send.at[i], recv_sem=na_recv.at[i],
            device_id={"rep": partner}, device_id_type=MESH,
        )
        c.start()
        na_out.append(c)

    for d in range(1, peers):
        src = lax.rem(me + d, peers)
        pltpu.make_async_remote_copy(
            src_ref=gathered.at[src], dst_ref=gathered.at[src],
            send_sem=s_send.at[d], recv_sem=s_recv.at[src],
            device_id={"fsdp": src}, device_id_type=MESH,
        ).wait_recv()
    for c in s_out:
        c.wait_send()
    t1, t2 = gathered[0, 0], gathered[0, 1]
    for d in range(1, peers):
        t1 = t1 + gathered[d, 0]
        t2 = t2 + gathered[d, 1]
    sums[0] = t1
    sums[1] = t2
    for c in bulk:
        c.wait()
    for i in range(chunks):
        w_out[i].wait_send()
        na_out[i].wait()


def adam_kernel(
    numel,
    step, na, nm, w, m, v, g1, g2, sums,
    na_out, nm_out, ni_out, nf_out, ns_out,
    ni, nf, ns, sem,
):
    na_copy = pltpu.make_async_copy(na, na_out, sem.at[0, 0])
    nm_copy = pltpu.make_async_copy(nm, nm_out, sem.at[1, 0])
    na_copy.start()
    nm_copy.start()
    rows, cols = w.shape

    def scalars(k):
        square_sum = jnp.sum(sums[k])
        norm = jnp.sqrt(jnp.full((8, 128), square_sum, jnp.float32))
        factor = jnp.minimum(1.0, 0.5 * math.sqrt(numel) / (norm + 1e-06))
        t = jnp.full((8, 128), 2 * step[0] + (k + 1), jnp.int32).astype(jnp.float32)
        b1 = 1.0 - jnp.exp(t * math.log(0.9))
        b2 = jnp.sqrt(1.0 - jnp.exp(t * math.log(0.95)))
        return (0.1 * factor)[0, 0], (0.1 * b2 / b1)[0, 0], (1e-08 * b2)[0, 0]

    h1, k1, e1 = scalars(0)
    h2, k2, e2 = scalars(1)
    k1 = k1 * 0.99

    triples = ((ni, ni_out), (nf, nf_out), (ns, ns_out))

    def copies(j):
        slot = lax.rem(j, SLOTS)
        rs = pl.ds(pl.multiple_of(j * ROWS, ROWS), ROWS)
        return [
            pltpu.make_async_copy(src.at[slot], dst.at[0, rs], sem.at[2 + k, slot])
            for k, (src, dst) in enumerate(triples)
        ]

    def body(j, carry):
        slot = lax.rem(j, SLOTS)

        @pl.when(j >= SLOTS)
        def _():
            for c in copies(j - SLOTS):
                c.wait()

        rs = pl.ds(pl.multiple_of(j * ROWS, ROWS), ROWS)
        for c in range(0, cols, COLS):
            cs = slice(c, c + COLS)
            x = h1 * g1[rs, cs].astype(jnp.float32)
            mm = 0.9 * m[rs, cs] + x
            vv = 0.95 * v[rs, cs] + 5.0 * (x * x)
            d = vv * lax.rsqrt(vv) + e1
            up = (k1 * mm) * lax.rsqrt(d * d)
            x = h2 * g2[rs, cs].astype(jnp.float32)
            mm = 0.9 * mm + x
            vv = 0.95 * vv + 5.0 * (x * x)
            nf[slot, :, cs] = mm
            ns[slot, :, cs] = vv
            d = vv * lax.rsqrt(vv) + e2
            up = up + (k2 * mm) * lax.rsqrt(d * d)
            ni[slot, :, cs] = na[rs, cs] - (0.0199 * w[rs, cs] + up)
        for c in copies(j):
            c.start()
        return carry

    steps = rows // ROWS
    lax.fori_loop(0, steps, body, 0)
    for j in range(max(0, steps - SLOTS), steps):
        for c in copies(j):
            c.wait()
    na_copy.wait()
    nm_copy.wait()


def fused(
    numel, peers,
    anchor, momentum, inner_weight, first_moment, second_moment, grad_first, grad_second, outer_step,
):
    rows, cols = anchor.shape
    half = momentum.shape[1]
    chunks = rows // CHUNK
    f32, bf16 = jnp.float32, jnp.bfloat16
    hbm = pl.BlockSpec(memory_space=pl.ANY)
    vmem = pl.BlockSpec(memory_space=pltpu.VMEM)
    dma = pltpu.SemaphoreType.DMA
    held = pl.pallas_call(
        functools.partial(exchange_kernel, peers),
        name="exchange",
        out_shape=[
            pltpu.VMEM((rows, cols), f32),
            pltpu.VMEM((rows, half), f32),
            pltpu.VMEM((rows, cols), f32),
            pltpu.VMEM((rows, cols), f32),
            pltpu.VMEM((rows, cols), f32),
            pltpu.VMEM((rows, cols), bf16),
            pltpu.VMEM((rows, cols), bf16),
            pltpu.VMEM((2, 8, 128), f32),
        ],
        in_specs=[hbm] * 7,
        out_specs=[vmem] * 8,
        scratch_shapes=[
            pltpu.VMEM((rows, half), f32),
            pltpu.VMEM((peers, 2, 8, 128), f32),
            dma((chunks,)), dma((chunks,)), dma((chunks,)), dma((chunks,)), dma((chunks,)),
            dma((3,)),
            dma((chunks,)), dma((chunks,)), dma((chunks,)), dma((chunks,)),
            dma((peers,)), dma((peers,)),
        ],
        compiler_params=pltpu.CompilerParams(
            collective_id=0, has_side_effects=True, vmem_limit_bytes=VMEM_A
        ),
    )(anchor, momentum, inner_weight, first_moment, second_moment, grad_first, grad_second)
    out = jax.ShapeDtypeStruct
    return pl.pallas_call(
        functools.partial(adam_kernel, numel),
        name="adam",
        out_shape=[
            out((rows, cols), f32),
            out((rows, half), f32),
            out((1, rows, cols), f32),
            out((1, rows, cols), f32),
            out((1, rows, cols), f32),
        ],
        in_specs=[pl.BlockSpec(memory_space=pltpu.SMEM)] + [vmem] * 8,
        out_specs=[hbm] * 5,
        scratch_shapes=[pltpu.VMEM((SLOTS, ROWS, cols), f32)] * 3 + [dma((5, SLOTS))],
        compiler_params=pltpu.CompilerParams(vmem_limit_bytes=VMEM_B),
    )(outer_step, *(pltpu.with_memory_space_constraint(x, pltpu.VMEM) for x in held))


VMEM_A = 8 << 20
VMEM_B = 8 << 20


def solution(mesh):
    in_specs = (
        P("fsdp", None),
        P("fsdp", "rep"),
        P("rep", "fsdp", None),
        P("rep", "fsdp", None),
        P("rep", "fsdp", None),
        P("rep", "fsdp", None),
        P("rep", "fsdp", None),
        P(),
    )
    out_specs = (
        P("fsdp", None),
        P("fsdp", "rep"),
        P("rep", "fsdp", None),
        P("rep", "fsdp", None),
        P("rep", "fsdp", None),
    )
    reps, peers = mesh.shape["rep"], mesh.shape["fsdp"]

    def on_device(*args):
        rows, cols = args[0].shape
        if reps == 2 and rows % CHUNK == 0 and cols % (2 * COLS) == 0:
            return tuple(fused(rows * peers * cols, peers, *args))
        return plain(*args)

    return jax.shard_map(
        on_device, mesh=mesh, in_specs=in_specs, out_specs=out_specs, check_vma=False
    )
```

```python
import functools
import math

import jax
import jax.numpy as jnp
from jax import lax
from jax.experimental import pallas as pl
from jax.experimental.pallas import tpu as pltpu
from jax.sharding import PartitionSpec as P

D = 3584
FF = 7168
CHUNK = 32
ROWS = 16
COLS = 256
SLOTS = 4
MESH = pl.DeviceIdType.MESH


def adam_apply(weight, first_moment, second_moment, grad_full, square_sum, step_count):
    factor = jnp.minimum(1.0, 0.5 * math.sqrt(D * FF) / (jnp.sqrt(square_sum) + 1e-06))
    scaled = factor * grad_full
    first_moment = 0.9 * first_moment + 0.1 * scaled
    second_moment = 0.95 * second_moment + 0.05 * scaled * scaled
    first_hat = first_moment / (1.0 - jnp.power(jnp.float32(0.9), step_count))
    second_hat = second_moment / (1.0 - jnp.power(jnp.float32(0.95), step_count))
    weight = weight - 0.1 * (first_hat / (jnp.sqrt(second_hat) + 1e-08) + 0.1 * weight)
    return (weight, first_moment, second_moment)


def outer_update(anchor, momentum, inner_weight):
    replicas = lax.axis_size("rep")
    col_count = momentum.shape[1]
    col_start = lax.axis_index("rep") * col_count
    pseudo = anchor - inner_weight[0]
    pseudo_sum = lax.psum(pseudo, "rep")
    full_momentum = lax.all_gather(momentum, "rep", axis=1, tiled=True)
    outer_grad = pseudo_sum / replicas
    momentum_full = 0.9 * full_momentum + outer_grad
    next_anchor = anchor - 0.7 * (outer_grad + 0.9 * momentum_full)
    next_momentum = lax.dynamic_slice_in_dim(momentum_full, col_start, col_count, 1)
    return (next_anchor, next_momentum)


def inner_steps(inner_weight, first_moment, second_moment, grad_first, grad_second, outer_step):
    base_step = 2 * outer_step[0]
    grad_one = grad_first[0].astype(jnp.float32)
    grad_two = grad_second[0].astype(jnp.float32)
    weight, moment_one, moment_two = (inner_weight[0], first_moment[0], second_moment[0])
    for offset, grad_full in ((1, grad_one), (2, grad_two)):
        square_sum = lax.psum(jnp.sum(grad_full * grad_full), "fsdp")
        weight, moment_one, moment_two = adam_apply(
            weight,
            moment_one,
            moment_two,
            grad_full,
            square_sum,
            (base_step + offset).astype(jnp.float32),
        )
    return (weight, moment_one, moment_two)


def plain(
    anchor, momentum, inner_weight, first_moment, second_moment, grad_first, grad_second, outer_step
):
    weight, moment_one, moment_two = inner_steps(
        inner_weight, first_moment, second_moment, grad_first, grad_second, outer_step
    )
    next_anchor, next_momentum = outer_update(anchor, momentum, inner_weight)
    next_inner = (next_anchor + (weight - inner_weight[0]))[None]
    return (next_anchor, next_momentum, next_inner, moment_one[None], moment_two[None])


def exchange_kernel(
    peers,
    anchor, momentum, inner, first, second, grad_one, grad_two,
    na, nm, w, m, v, g1, g2, sums,
    other_w, gathered,
    g1_sem, g2_sem, a_sem, w_sem, mom_sem, bulk_sem,
    w_send, w_recv, na_send, na_recv, s_send, s_recv,
):
    rows, half = momentum.shape
    chunks = rows // CHUNK
    me = lax.axis_index("fsdp")
    rep = lax.axis_index("rep")
    partner = 1 - rep
    own = pl.ds(pl.multiple_of(rep * half, 128), half)
    far = pl.ds(pl.multiple_of(partner * half, 128), half)

    def cut(i):
        return pl.ds(i * CHUNK, CHUNK)

    barrier = pltpu.get_barrier_semaphore()
    pl.semaphore_signal(barrier, inc=1, device_id={"rep": partner}, device_id_type=MESH)
    for d in range(1, peers):
        pl.semaphore_signal(
            barrier, inc=1, device_id={"fsdp": lax.rem(me + d, peers)}, device_id_type=MESH
        )

    g1_in = [pltpu.make_async_copy(grad_one.at[0, cut(i)], g1.at[cut(i)], g1_sem.at[i]) for i in range(chunks)]
    g2_in = [pltpu.make_async_copy(grad_two.at[0, cut(i)], g2.at[cut(i)], g2_sem.at[i]) for i in range(chunks)]
    a_in = [pltpu.make_async_copy(anchor.at[cut(i), own], na.at[cut(i), own], a_sem.at[i]) for i in range(chunks)]
    w_in = [pltpu.make_async_copy(inner.at[0, cut(i), own], w.at[cut(i), own], w_sem.at[i]) for i in range(chunks)]
    mom_in = [pltpu.make_async_copy(momentum.at[cut(i)], nm.at[cut(i)], mom_sem.at[i]) for i in range(chunks)]
    bulk = [
        pltpu.make_async_copy(inner.at[0, :, far], w.at[:, far], bulk_sem.at[0]),
        pltpu.make_async_copy(first.at[0], m, bulk_sem.at[1]),
        pltpu.make_async_copy(second.at[0], v, bulk_sem.at[2]),
    ]
    for i in range(chunks):
        g1_in[i].start()
        g2_in[i].start()
    for i in range(chunks):
        a_in[i].start()
        w_in[i].start()
        mom_in[i].start()

    pl.semaphore_wait(barrier, peers)

    w_out = [
        pltpu.make_async_remote_copy(
            src_ref=inner.at[0, cut(i), far], dst_ref=other_w.at[cut(i)],
            send_sem=w_send.at[i], recv_sem=w_recv.at[i],
            device_id={"rep": partner}, device_id_type=MESH,
        )
        for i in range(chunks)
    ]
    for c in w_out:
        c.start()
    for c in bulk:
        c.start()

    lane = 128
    tiles = (2 * half) // lane
    total1 = total2 = jnp.zeros((8, lane), jnp.float32)
    for i in range(chunks):
        g1_in[i].wait()
        g2_in[i].wait()

        def square(j, carry):
            base = pl.multiple_of(i * CHUNK + j * ROWS, ROWS)
            accs = list(carry)
            for t in range(tiles):
                for k, ref in ((0, g1), (2, g2)):
                    x = ref[pl.ds(base, ROWS), t * lane:(t + 1) * lane].astype(jnp.float32)
                    x = x * x
                    accs[k] = accs[k] + x[:8]
                    accs[k + 1] = accs[k + 1] + x[8:]
            return tuple(accs)

        zero = jnp.zeros((8, lane), jnp.float32)
        accs = lax.fori_loop(0, CHUNK // ROWS, square, (zero,) * 4)
        total1 = total1 + (accs[0] + accs[1])
        total2 = total2 + (accs[2] + accs[3])

    gathered[me, 0] = total1
    gathered[me, 1] = total2
    s_out = []
    for d in range(1, peers):
        c = pltpu.make_async_remote_copy(
            src_ref=gathered.at[me], dst_ref=gathered.at[me],
            send_sem=s_send.at[d], recv_sem=s_recv.at[me],
            device_id={"fsdp": lax.rem(me + d, peers)}, device_id_type=MESH,
        )
        c.start()
        s_out.append(c)

    na_out = []
    for i in range(chunks):
        a_in[i].wait()
        w_in[i].wait()
        mom_in[i].wait()
        w_out[i].wait_recv()

        def outer(j, carry):
            base = pl.multiple_of(i * CHUNK + j * 8, 8)
            rs = pl.ds(base, 8)
            for t in range(0, half, COLS):
                cs = pl.ds(pl.multiple_of(rep * half + t, 128), COLS)
                a = na[rs, cs]
                grad = ((a - w[rs, cs]) + (a - other_w[rs, t:t + COLS])) * 0.5
                mom = 0.9 * nm[rs, t:t + COLS] + grad
                nm[rs, t:t + COLS] = mom
                na[rs, cs] = a - 0.7 * (grad + 0.9 * mom)
            return carry

        lax.fori_loop(0, CHUNK // 8, outer, 0)
        c = pltpu.make_async_remote_copy(
            src_ref=na.at[cut(i), own], dst_ref=na.at[cut(i), own],
            send_sem=na_send.at[i], recv_sem=na_recv.at[i],
            device_id={"rep": partner}, device_id_type=MESH,
        )
        c.start()
        na_out.append(c)

    for d in range(1, peers):
        src = lax.rem(me + d, peers)
        pltpu.make_async_remote_copy(
            src_ref=gathered.at[src], dst_ref=gathered.at[src],
            send_sem=s_send.at[d], recv_sem=s_recv.at[src],
            device_id={"fsdp": src}, device_id_type=MESH,
        ).wait_recv()
    for c in s_out:
        c.wait_send()
    t1, t2 = gathered[0, 0], gathered[0, 1]
    for d in range(1, peers):
        t1 = t1 + gathered[d, 0]
        t2 = t2 + gathered[d, 1]
    sums[0] = t1
    sums[1] = t2
    for c in bulk:
        c.wait()
    for i in range(chunks):
        w_out[i].wait_send()
        na_out[i].wait()


def adam_kernel(
    numel,
    step, na, nm, w, m, v, g1, g2, sums,
    na_out, nm_out, ni_out, nf_out, ns_out,
    ni, nf, ns, sem,
):
    na_copy = pltpu.make_async_copy(na, na_out, sem.at[0, 0])
    nm_copy = pltpu.make_async_copy(nm, nm_out, sem.at[1, 0])
    na_copy.start()
    nm_copy.start()
    rows, cols = w.shape

    def scalars(k):
        square_sum = jnp.sum(sums[k])
        norm = jnp.sqrt(jnp.full((8, 128), square_sum, jnp.float32))
        factor = jnp.minimum(1.0, 0.5 * math.sqrt(numel) / (norm + 1e-06))
        t = jnp.full((8, 128), 2 * step[0] + (k + 1), jnp.int32).astype(jnp.float32)
        b1 = 1.0 - jnp.exp(t * math.log(0.9))
        b2 = jnp.sqrt(1.0 - jnp.exp(t * math.log(0.95)))
        return (0.1 * factor)[0, 0], (0.1 * b2 / b1)[0, 0], (1e-08 * b2)[0, 0]

    h1, k1, e1 = scalars(0)
    h2, k2, e2 = scalars(1)
    k1 = k1 * 0.99

    triples = ((ni, ni_out), (nf, nf_out), (ns, ns_out))

    def copies(j):
        slot = lax.rem(j, SLOTS)
        rs = pl.ds(pl.multiple_of(j * ROWS, ROWS), ROWS)
        return [
            pltpu.make_async_copy(src.at[slot], dst.at[0, rs], sem.at[2 + k, slot])
            for k, (src, dst) in enumerate(triples)
        ]

    def body(j, carry):
        slot = lax.rem(j, SLOTS)

        @pl.when(j >= SLOTS)
        def _():
            for c in copies(j - SLOTS):
                c.wait()

        rs = pl.ds(pl.multiple_of(j * ROWS, ROWS), ROWS)
        for c in range(0, cols, COLS):
            cs = slice(c, c + COLS)
            x = h1 * g1[rs, cs].astype(jnp.float32)
            mm = 0.9 * m[rs, cs] + x
            vv = 0.95 * v[rs, cs] + 5.0 * (x * x)
            d = vv * lax.rsqrt(vv) + e1
            up = (k1 * mm) * lax.rsqrt(d * d)
            x = h2 * g2[rs, cs].astype(jnp.float32)
            mm = 0.9 * mm + x
            vv = 0.95 * vv + 5.0 * (x * x)
            nf[slot, :, cs] = mm
            ns[slot, :, cs] = vv
            d = vv * lax.rsqrt(vv) + e2
            up = up + (k2 * mm) * lax.rsqrt(d * d)
            ni[slot, :, cs] = na[rs, cs] - (0.0199 * w[rs, cs] + up)
        for c in copies(j):
            c.start()
        return carry

    steps = rows // ROWS
    lax.fori_loop(0, steps, body, 0)
    for j in range(max(0, steps - SLOTS), steps):
        for c in copies(j):
            c.wait()
    na_copy.wait()
    nm_copy.wait()


def fused(
    numel, peers,
    anchor, momentum, inner_weight, first_moment, second_moment, grad_first, grad_second, outer_step,
):
    rows, cols = anchor.shape
    half = momentum.shape[1]
    chunks = rows // CHUNK
    f32, bf16 = jnp.float32, jnp.bfloat16
    hbm = pl.BlockSpec(memory_space=pl.ANY)
    vmem = pl.BlockSpec(memory_space=pltpu.VMEM)
    dma = pltpu.SemaphoreType.DMA
    held = pl.pallas_call(
        functools.partial(exchange_kernel, peers),
        name="exchange",
        out_shape=[
            pltpu.VMEM((rows, cols), f32),
            pltpu.VMEM((rows, half), f32),
            pltpu.VMEM((rows, cols), f32),
            pltpu.VMEM((rows, cols), f32),
            pltpu.VMEM((rows, cols), f32),
            pltpu.VMEM((rows, cols), bf16),
            pltpu.VMEM((rows, cols), bf16),
            pltpu.VMEM((2, 8, 128), f32),
        ],
        in_specs=[hbm] * 7,
        out_specs=[vmem] * 8,
        scratch_shapes=[
            pltpu.VMEM((rows, half), f32),
            pltpu.VMEM((peers, 2, 8, 128), f32),
            dma((chunks,)), dma((chunks,)), dma((chunks,)), dma((chunks,)), dma((chunks,)),
            dma((3,)),
            dma((chunks,)), dma((chunks,)), dma((chunks,)), dma((chunks,)),
            dma((peers,)), dma((peers,)),
        ],
        compiler_params=pltpu.CompilerParams(
            collective_id=0, has_side_effects=True, vmem_limit_bytes=VMEM_A
        ),
    )(*(pltpu.with_memory_space_constraint(x, pltpu.HBM) for x in (
        anchor, momentum, inner_weight, first_moment, second_moment, grad_first, grad_second
    )))
    out = jax.ShapeDtypeStruct
    return pl.pallas_call(
        functools.partial(adam_kernel, numel),
        name="adam",
        out_shape=[
            out((rows, cols), f32),
            out((rows, half), f32),
            out((1, rows, cols), f32),
            out((1, rows, cols), f32),
            out((1, rows, cols), f32),
        ],
        in_specs=[pl.BlockSpec(memory_space=pltpu.SMEM)] + [vmem] * 8,
        out_specs=[hbm] * 5,
        scratch_shapes=[pltpu.VMEM((SLOTS, ROWS, cols), f32)] * 3 + [dma((5, SLOTS))],
        compiler_params=pltpu.CompilerParams(vmem_limit_bytes=VMEM_B),
    )(outer_step, *(pltpu.with_memory_space_constraint(x, pltpu.VMEM) for x in held))


VMEM_A = 8 << 20
VMEM_B = 8 << 20


def solution(mesh):
    in_specs = (
        P("fsdp", None),
        P("fsdp", "rep"),
        P("rep", "fsdp", None),
        P("rep", "fsdp", None),
        P("rep", "fsdp", None),
        P("rep", "fsdp", None),
        P("rep", "fsdp", None),
        P(),
    )
    out_specs = (
        P("fsdp", None),
        P("fsdp", "rep"),
        P("rep", "fsdp", None),
        P("rep", "fsdp", None),
        P("rep", "fsdp", None),
    )
    reps, peers = mesh.shape["rep"], mesh.shape["fsdp"]

    def on_device(*args):
        rows, cols = args[0].shape
        if reps == 2 and rows % CHUNK == 0 and cols % (2 * COLS) == 0:
            return tuple(fused(rows * peers * cols, peers, *args))
        return plain(*args)

    return jax.shard_map(
        on_device, mesh=mesh, in_specs=in_specs, out_specs=out_specs, check_vma=False
    )
```
